32 devices in a mesh: groups: 2 (over y), seq: 8 (over z, x), head: 2 (over core).
Axes of the slice: x: 2, y: 2, z: 4, core: 2. Of those that a mesh axis runs over, the one named last changes fastest.
Arguments:
- tokens: bfloat16 [8192, 1024], P(('groups', 'seq')), parts along dimension 0, may hold values from -24 to 24
- w_qkv: bfloat16 [3, 1024, 512], P(None, None, 'head'), may hold values from -0.1875 to 0.1875
- w_out: bfloat16 [512, 1024], P('head'), may hold values from -0.25 to 0.25
- random_blocks: int32 [128, 3], P(('groups', 'seq')), parts along dimension 0, may hold values from 0 to 63, as said below
- global_ids: int32 [32], P('groups'), parts along dimension 0, may hold values from 0 to 63, as said below
Outputs:
- mixed: bfloat16 [8192, 1024], P(('groups', 'seq'), 'head'), parts along dimension 0
The draws below stay inside these ranges and needn't reach their ends.
There are 2 independent parts, one for each index of `groups`. The reference program is written for one: setup_inputs(seed, part) draws one part's arguments, and reference() takes and returns one part's arrays. A program takes and returns all parts, laid end to end along the dimension named above; an argument that names none is the same for every part. Nothing has to cross between parts.
Inputs may be any that keep to these rules, and one draw needn't show every extreme that they name: `random_blocks`: each entry of row b is a block of the document; its index of seq, entry // 8, lies within 1 places of b // 8 around the closed cycle of seq, and some entry of every draw lies exactly 1 places ahead and another exactly 1 places behind. `global_ids`: distinct block numbers.
All inputs are finite; a program needn't handle non-finite values.
Results may differ from the reference program's by a relative error of at most 0.011.
Values may be sent and summed in bfloat16 or wider, within the bound.
A program may use at most 64 MiB of HBM per device.

```python
import math
import jax
import jax.numpy as jnp
from jax import lax

D = 1024
HEADS = 8
HEAD_DIM = 64
BLOCK = 64
RAND = 3
BLK_DEV = 8
NBLOCKS = 64
TOKENS = 4096
GLOBALS = 16
REACH = 1


def draw_tokens(key, part):
    key = jax.random.fold_in(key, 5)
    first = jax.random.fold_in(key, 0)
    values = jnp.clip(jax.random.normal(first, (TOKENS, D), jnp.float32), -6.0, 6.0)
    return values.astype(jnp.bfloat16)


def draw_random_blocks(key, part):
    key = jax.random.fold_in(key, 11)
    first, second = jax.random.split(key)
    cycle_count = NBLOCKS // BLK_DEV
    offsets = jax.random.randint(first, (NBLOCKS, RAND), -REACH, REACH + 1)
    offsets = offsets.at[0, 0].set(REACH).at[0, 1].set(-REACH)
    inside_offset = jax.random.randint(second, (NBLOCKS, RAND), 0, BLK_DEV)
    owners = jnp.arange(NBLOCKS, dtype=jnp.int32) // BLK_DEV
    placed = (owners[:, None] + offsets) % cycle_count * BLK_DEV + inside_offset
    return placed.astype(jnp.int32)


def draw_global_ids(key, part):
    key = jax.random.fold_in(key, 17)
    ordering = jax.random.permutation(key, NBLOCKS)
    return ordering[:GLOBALS].astype(jnp.int32)


def level_of(own_key, dims, pieces, low, high):
    factor_of = 1.0
    for position, blocks in pieces:
        steps = jax.random.uniform(jax.random.fold_in(jax.random.fold_in(own_key, 6), position), (blocks,), jnp.float32, low / len(pieces), high / len(pieces))
        factor_of = factor_of * jnp.repeat(jnp.exp(steps), dims[position] // blocks).reshape((-1,) + (1,) * (len(dims) - 1 - position))
    return factor_of


def gaussian(own_key, extent, spread, bound, cuts=(), kind=jnp.bfloat16):
    array = spread * jax.random.normal(own_key, extent, jnp.float32)
    if cuts:
        array = array * level_of(own_key, extent, cuts, -0.22, 0.18)
    return jnp.clip(array, -bound, bound).astype(kind)


def setup_inputs(seed: int = 0, part: int = 0) -> dict:
    key_of = jax.random.split(jax.random.key(seed), 6)
    part_splits = jax.random.split(jax.random.fold_in(key_of[5], part), 6)
    return {
        "tokens": draw_tokens(jax.random.fold_in(jax.random.fold_in(key_of[5], part), 71), part),
        "w_qkv": gaussian(key_of[1], (3, D, HEADS * HEAD_DIM), D ** -0.5, 0.1875, ((2, 2),)),
        "w_out": gaussian(key_of[2], (HEADS * HEAD_DIM, D), (HEADS * HEAD_DIM) ** -0.5, 0.25, ((0, 2),)),
        "random_blocks": draw_random_blocks(jax.random.fold_in(jax.random.fold_in(key_of[5], part), 71), part),
        "global_ids": draw_global_ids(jax.random.fold_in(jax.random.fold_in(key_of[5], part), 71), part),
    }


def reference(tokens, w_qkv, w_out, random_blocks, global_ids):
    blk_total = tokens.shape[0] // BLOCK
    scale_factor = 1.0 / math.sqrt(HEAD_DIM)
    projected = [jnp.dot(tokens, w_qkv[index], preferred_element_type=jnp.float32).astype(jnp.bfloat16) for index in range(3)]
    queries = projected[0].reshape(blk_total, BLOCK, HEADS, HEAD_DIM)
    key_rows = projected[1].reshape(blk_total, BLOCK, HEADS, HEAD_DIM)
    value_rows = projected[2].reshape(blk_total, BLOCK, HEADS, HEAD_DIM)

    def attend_block(block_id):
        neighbours = jnp.stack([(block_id - 1) % blk_total, block_id, (block_id + 1) % blk_total]).astype(jnp.int32)
        chosen = jnp.concatenate([neighbours, random_blocks[block_id].astype(jnp.int32), global_ids.astype(jnp.int32)])
        keys_here = key_rows[chosen].reshape(-1, HEADS, HEAD_DIM).astype(jnp.float32)
        vals_here = value_rows[chosen].reshape(-1, HEADS, HEAD_DIM).astype(jnp.float32)
        scores = jnp.einsum('qhd,khd->hqk', queries[block_id].astype(jnp.float32), keys_here) * scale_factor
        largest = lax.optimization_barrier(jnp.max(scores, axis=-1, keepdims=True))
        raw_weights = jnp.exp(scores - largest)
        totals = lax.optimization_barrier(jnp.sum(raw_weights, axis=-1, keepdims=True))
        weights = (raw_weights / totals).astype(jnp.bfloat16)
        blended = jnp.einsum('hqk,khd->qhd', weights.astype(jnp.float32), vals_here)
        return blended.astype(jnp.bfloat16).reshape(BLOCK, HEADS * HEAD_DIM)
    attention = lax.map(attend_block, jnp.arange(blk_total, dtype=jnp.int32)).reshape(-1, HEADS * HEAD_DIM)
    return jnp.dot(attention, w_out, preferred_element_type=jnp.float32).astype(jnp.bfloat16)
```

```python
import math

import jax
import jax.numpy as jnp
from jax import lax
from jax.experimental import pallas as pl
from jax.experimental.pallas import tpu as pltpu
from jax.sharding import PartitionSpec as P

HEAD_DIM = 64
BLOCK = 64
RAND = 3
MESH = pl.DeviceIdType.MESH


def padded_2(block, sides, width):
    for axis, dim in sides:
        count = lax.axis_size(axis)
        forward = [(i, i + 1) for i in range(count - 1)]
        forward.append((count - 1, 0))
        backward = [(target, source) for source, target in forward]
        low = lax.ppermute(
            lax.slice_in_dim(block, block.shape[dim] - width, None, axis=dim), axis, forward
        )
        high = lax.ppermute(lax.slice_in_dim(block, 0, width, axis=dim), axis, backward)
        block = jnp.concatenate([low, block, high], axis=dim)
    return block


def passed_along(block, axis, distance):
    devices = range(lax.axis_size(axis))
    route = [((i - distance) % len(devices), i) for i in devices]
    return lax.ppermute(block, axis, route)


def broadcast(shard, axis, root):
    mine = lax.axis_index(axis) == root
    return lax.psum(jnp.where(mine, shard, jnp.zeros_like(shard)), axis)


def attend_head(packed):
    single_query_head, local_block_pair, global_block_pair = packed
    scale_factor = 1.0 / math.sqrt(single_query_head.shape[-1])
    local_scores = (
        jnp.einsum(
            "vhw,vcw->vhc",
            single_query_head,
            local_block_pair[0],
            preferred_element_type=jnp.float32,
        )
        * scale_factor
    )
    global_scores = (
        jnp.einsum(
            "ors,is->ori",
            single_query_head,
            global_block_pair[0],
            preferred_element_type=jnp.float32,
        )
        * scale_factor
    )
    largest = jnp.maximum(
        jnp.max(local_scores, axis=-1, keepdims=True),
        jnp.max(global_scores, axis=-1, keepdims=True),
    )
    local_exp = jnp.exp(local_scores - largest)
    global_exp = jnp.exp(global_scores - largest)
    totals = jnp.sum(local_exp, axis=-1, keepdims=True) + jnp.sum(
        global_exp, axis=-1, keepdims=True
    )
    local_attention_weights = (local_exp / totals).astype(jnp.bfloat16)
    global_attention_weights = (global_exp / totals).astype(jnp.bfloat16)
    blended = jnp.einsum(
        "onw,owz->onz",
        local_attention_weights,
        local_block_pair[1],
        preferred_element_type=jnp.float32,
    )
    blended = blended + jnp.einsum(
        "sou,ug->sog",
        global_attention_weights,
        global_block_pair[1],
        preferred_element_type=jnp.float32,
    )
    return blended.astype(jnp.bfloat16)


def on_device(tokens, w_qkv, w_out, random_blocks, global_ids):
    cycle_size = lax.axis_size("seq")
    my_index = lax.axis_index("seq")
    reach_count = max(1, cycle_size // 64)
    tok_rows = tokens.shape[0]
    blk_count = tok_rows // BLOCK
    features = w_qkv.shape[2]
    head_count = features // HEAD_DIM
    queries = jnp.dot(tokens, w_qkv[0], preferred_element_type=jnp.float32).astype(jnp.bfloat16)
    key_rows = jnp.dot(tokens, w_qkv[1], preferred_element_type=jnp.float32).astype(jnp.bfloat16)
    value_rows = jnp.dot(tokens, w_qkv[2], preferred_element_type=jnp.float32).astype(jnp.bfloat16)
    paired_blocks = jnp.stack([key_rows, value_rows])
    pair_blocks = paired_blocks.reshape(2, blk_count, BLOCK, features)
    padded = padded_2(paired_blocks, (("seq", 1),), BLOCK)
    padded_blocks = padded.reshape(2, blk_count + 2, BLOCK, features)
    window = jnp.concatenate(
        [
            padded_blocks[:, 0:blk_count],
            padded_blocks[:, 1 : blk_count + 1],
            padded_blocks[:, 2 : blk_count + 2],
        ],
        axis=2,
    )
    flat_lists = random_blocks.reshape(-1)
    list_owner = flat_lists // blk_count
    list_within = flat_lists % blk_count
    relative = (list_owner - my_index) % cycle_size

    def pick_blocks(collected, piece, offset):
        taken = jnp.take(piece, list_within, axis=1)
        matches = relative == offset % cycle_size
        return jnp.where(matches[None, :, None, None], taken, collected)

    collected = jnp.zeros((2, blk_count * RAND, BLOCK, features), jnp.bfloat16)
    current = passed_along(pair_blocks, "seq", -reach_count)
    collected = pick_blocks(collected, current, reach_count)

    def advance(turn_index, carried):
        moving, gathered = carried
        moving = passed_along(moving, "seq", 1)
        return (moving, pick_blocks(gathered, moving, reach_count - turn_index))

    current, collected = lax.fori_loop(1, 2 * reach_count + 1, advance, (current, collected))
    global_owner = global_ids // blk_count
    global_within = global_ids % blk_count
    global_count = global_ids.shape[0]

    def fetch_global(slot_index, gathered):
        local_piece = lax.dynamic_index_in_dim(
            pair_blocks, global_within[slot_index], axis=1, keepdims=False
        )
        arrived = broadcast(local_piece, "seq", global_owner[slot_index])
        return lax.dynamic_update_index_in_dim(gathered, arrived, slot_index, axis=1)

    global_block_pair = lax.fori_loop(
        0, global_count, fetch_global, jnp.zeros((2, global_count, BLOCK, features), jnp.bfloat16)
    )
    local_block_pair = jnp.concatenate(
        [window, collected.reshape(2, blk_count, RAND * BLOCK, features)], axis=2
    )
    local_heads = local_block_pair.reshape(2, blk_count, -1, head_count, HEAD_DIM).transpose(
        3, 0, 1, 2, 4
    )
    global_heads = global_block_pair.reshape(
        2, global_count * BLOCK, head_count, HEAD_DIM
    ).transpose(2, 0, 1, 3)
    query_heads = queries.reshape(blk_count, BLOCK, head_count, HEAD_DIM).transpose(2, 0, 1, 3)
    attended = lax.map(attend_head, (query_heads, local_heads, global_heads))
    attention = attended.transpose(1, 2, 0, 3).reshape(tok_rows, features)
    partial_sum = jnp.dot(attention, w_out, preferred_element_type=jnp.float32)
    return lax.psum_scatter(
        partial_sum.astype(jnp.bfloat16), "head", scatter_dimension=1, tiled=True
    )


def route_kernel(rand_ref, gid_ref, tok_ref, wqkv_ref, wout_ref, out_ref,
                 krow, vrow, kz, vz, q_ref, gk, gv, near_k, near_v, far_k, far_v,
                 nsend_k, nsend_v, fsend_k, fsend_v, wfull, att,
                 xs, xr, zs, zr, ns, nr, fs, fr, gs, gr, ws, wr, hs, hr):
    rows = tok_ref.shape[0]
    feats = wqkv_ref.shape[2]
    half_out = out_ref.shape[1]
    blocks = rows // BLOCK
    pair = 2 * blocks
    heads = feats // HEAD_DIM
    slots = gid_ref.shape[0]
    mine = slots // 2
    me = lax.axis_index("seq")
    core = lax.axis_index("head")
    cycle = lax.axis_size("seq")
    lines = cycle // 2
    z = me // 2
    x = me % 2
    partner = z * 2 + (1 - x)
    z_next = ((z + 1) % lines) * 2 + x
    z_prev = ((z + lines - 1) % lines) * 2 + x
    to_near = ((z + 1 + (lines - 2) * x) % lines) * 2 + x
    side = (z * 2) // lines
    ahead = z + 1 - 2 * side
    behind = (z + lines - 1 + 2 * side) % lines
    inner = jnp.logical_and(z > 0, z < lines - 1)
    fwd_dev = ahead * 2 + x
    back_dev = behind * 2 + x

    barrier = pltpu.get_barrier_semaphore()
    for who in ({"seq": partner}, {"seq": z_next}, {"seq": z_prev}, {"head": 1 - core}):
        pl.semaphore_signal(barrier, inc=1, device_id=who, device_id_type=MESH)

    def remote(src, dst, ssem, rsem, who):
        return pltpu.make_async_remote_copy(
            src_ref=src, dst_ref=dst, send_sem=ssem, recv_sem=rsem,
            device_id=who, device_id_type=MESH)

    here = pl.ds(pl.multiple_of(x * rows, rows), rows)
    there = pl.ds(pl.multiple_of((1 - x) * rows, rows), rows)

    def project(index):
        return jnp.dot(tok_ref[...], wqkv_ref[index],
                       preferred_element_type=jnp.float32).astype(jnp.bfloat16)

    krow[here, :] = project(1)
    pl.semaphore_wait(barrier, 4)
    send_x = [remote(buf.at[here], buf.at[here], xs.at[i], xr.at[i], {"seq": partner})
              for i, buf in enumerate((krow, vrow))]
    got_x = [remote(buf.at[there], buf.at[there], xs.at[i], xr.at[i], {"seq": partner})
             for i, buf in enumerate((krow, vrow))]
    send_x[0].start()
    vrow[here, :] = project(2)
    send_x[1].start()
    wmine = pl.ds(pl.multiple_of(core * feats, feats), feats)
    wother = pl.ds(pl.multiple_of((1 - core) * feats, feats), feats)
    send_w = remote(
        wout_ref.at[:, pl.ds(pl.multiple_of((1 - core) * half_out, half_out), half_out)],
        wfull.at[wmine], ws.at[0], wr.at[0], {"head": 1 - core})
    send_w.start()
    wfull[wmine, :] = wout_ref[:, pl.ds(pl.multiple_of(core * half_out, half_out), half_out)]
    q_ref[...] = project(0)

    near = (near_k, near_v)
    far = (far_k, far_v)
    nsend = (nsend_k, nsend_v)
    fsend = (fsend_k, fsend_v)
    row = (krow, vrow)
    zbuf = (kz, vz)
    gbuf = (gk, gv)

    def near_copy(kind, j, crossing):
        part = pl.ds(j * BLOCK, BLOCK)
        n = kind * mine + j
        dst, sem = (far, fr) if crossing else (near, nr)
        return remote(nsend[kind].at[part], dst[kind].at[part], ns.at[n], sem.at[n],
                      {"seq": fwd_dev})

    def far_copy(kind, j):
        part = pl.ds(j * BLOCK, BLOCK)
        n = kind * mine + j
        return remote(fsend[kind].at[part], far[kind].at[part], fs.at[n], fr.at[n],
                      {"seq": back_dev})

    def owner(j):
        gid = gid_ref[x * mine + j]
        return lax.div(gid, pair), lax.rem(gid, pair)

    def step_near(kind, j):
        part = pl.ds(j * BLOCK, BLOCK)
        line, within = owner(j)
        own = row[kind][pl.ds(within * BLOCK, BLOCK), :]

        @pl.when(inner)
        def _():
            near_copy(kind, j, False).wait_recv()
            nsend[kind][part, :] = jnp.where(line == z, own, near[kind][part, :])
            near_copy(kind, j, True).start()

        @pl.when(jnp.logical_not(inner))
        def _():
            nsend[kind][part, :] = own
            near_copy(kind, j, False).start()

    def g_copy(kind, j):
        spot = pl.ds(pl.multiple_of((x * mine + j) * BLOCK, BLOCK), BLOCK)
        n = kind * mine + j
        return remote(gbuf[kind].at[spot], gbuf[kind].at[spot], gs.at[n], gr.at[n],
                      {"seq": partner})

    def step_far(kind, j):
        part = pl.ds(j * BLOCK, BLOCK)
        spot = pl.ds(pl.multiple_of((x * mine + j) * BLOCK, BLOCK), BLOCK)
        line, within = owner(j)
        own = row[kind][pl.ds(within * BLOCK, BLOCK), :]
        far_copy(kind, j).wait_recv()
        arrived = far[kind][part, :]

        @pl.when(inner)
        def _():
            fsend[kind][part, :] = jnp.where(line == z, own, arrived)
            far_copy(kind, j).start()
            before = jnp.where(side == 0, line < z, line > z)
            gbuf[kind][spot, :] = jnp.where(
                line == z, own, jnp.where(before, near[kind][part, :], arrived))

        @pl.when(jnp.logical_not(inner))
        def _():
            gbuf[kind][spot, :] = jnp.where(line == z, own, arrived)

        g_copy(kind, j).start()

    send_z = [remote(row[i].at[there], zbuf[i], zs.at[i], zr.at[i], {"seq": to_near})
              for i in range(2)]

    lag = 3
    total = 2 * mine
    for t in range(total + lag):
        if t < total:
            kind, j = t // mine, t % mine
            if j == 0:
                got_x[kind].wait_recv()
            step_near(kind, j)
            if j == mine - 1:
                send_z[kind].start()
        if t >= lag:
            u = t - lag
            step_far(u // mine, u % mine)

    for kind in range(2):
        for j in range(mine):
            n = kind * mine + j
            spot = pl.ds(pl.multiple_of(((1 - x) * mine + j) * BLOCK, BLOCK), BLOCK)
            remote(gbuf[kind].at[spot], gbuf[kind].at[spot], gs.at[n], gr.at[n],
                   {"seq": partner}).wait_recv()
    for kind in range(2):
        send_z[kind].wait_recv()

    lane_head = lax.broadcasted_iota(jnp.int32, (BLOCK, feats), 1) // HEAD_DIM
    masks = [(lane_head == h).astype(jnp.float32) for h in range(heads)]
    masks16 = [m.astype(jnp.bfloat16) for m in masks]
    factor = math.log2(math.e) / math.sqrt(HEAD_DIM)
    doc_blocks = cycle * blocks

    def fetch(bufs, e):
        place = e - pair * z
        inside = jnp.logical_and(place >= 0, place < pair)
        place = jnp.clip(place, 0, pair - 1)
        a = bufs[0][pl.ds(place * BLOCK, BLOCK), :]
        b = bufs[1][pl.ds(lax.rem(e, blocks) * BLOCK, BLOCK), :]
        return jnp.where(inside, a, b)

    def att_copy(b):
        spot = pl.ds(pl.multiple_of(b * BLOCK, BLOCK), BLOCK)
        return remote(att.at[core, spot], att.at[core, spot], hs.at[b], hr.at[b],
                      {"head": 1 - core})

    def one_block(b, carry):
        spot = pl.ds(pl.multiple_of(b * BLOCK, BLOCK), BLOCK)
        q = q_ref[spot, :]
        stacked = jnp.concatenate([q * m for m in masks16], axis=0)
        mid = me * blocks + b
        picks = [lax.rem(mid + doc_blocks - 1, doc_blocks), mid,
                 lax.rem(mid + 1, doc_blocks)] + [rand_ref[b, i] for i in range(RAND)]
        kloc = jnp.concatenate([fetch((krow, kz), e) for e in picks], axis=0)
        vloc = jnp.concatenate([fetch((vrow, vz), e) for e in picks], axis=0)
        dims = (((1,), (1,)), ((), ()))
        sl = lax.dot_general(stacked, kloc, dims, preferred_element_type=jnp.float32)
        sg = lax.dot_general(stacked, gk[...], dims, preferred_element_type=jnp.float32)
        top = jnp.maximum(jnp.max(sl, axis=1, keepdims=True), jnp.max(sg, axis=1, keepdims=True))
        el = jnp.exp2((sl - top) * factor)
        eg = jnp.exp2((sg - top) * factor)
        norm = jnp.sum(el, axis=1, keepdims=True) + jnp.sum(eg, axis=1, keepdims=True)
        o = jnp.dot(el.astype(jnp.bfloat16), vloc, preferred_element_type=jnp.float32)
        o += jnp.dot(eg.astype(jnp.bfloat16), gv[...], preferred_element_type=jnp.float32)
        o = o / norm
        merged = o[0:BLOCK] * masks[0]
        for h in range(1, heads):
            merged += o[h * BLOCK:(h + 1) * BLOCK] * masks[h]
        att[core, spot, :] = merged.astype(jnp.bfloat16)
        att_copy(b).start()
        return carry

    lax.fori_loop(0, blocks, one_block, 0)

    remote(wout_ref.at[:, pl.ds(0, half_out)], wfull.at[wother], ws.at[0], wr.at[0],
           {"head": 1 - core}).wait_recv()
    acc = jnp.dot(att[core], wfull[wmine, :], preferred_element_type=jnp.float32)

    def other_in(b, carry):
        spot = pl.ds(pl.multiple_of(b * BLOCK, BLOCK), BLOCK)
        remote(att.at[1 - core, spot], att.at[1 - core, spot], hs.at[b], hr.at[b],
               {"head": 1 - core}).wait_recv()
        return carry

    lax.fori_loop(0, blocks, other_in, 0)
    acc += jnp.dot(att[1 - core], wfull[wother, :], preferred_element_type=jnp.float32)
    out_ref[...] = acc.astype(jnp.bfloat16)

    for kind in range(2):
        send_x[kind].wait_send()
        send_z[kind].wait_send()
        for j in range(mine):
            near_copy(kind, j, False).wait_send()
            g_copy(kind, j).wait_send()
    send_w.wait_send()

    @pl.when(inner)
    def _():
        for kind in range(2):
            for j in range(mine):
                far_copy(kind, j).wait_send()

    def sent(b, carry):
        att_copy(b).wait_send()
        return carry

    lax.fori_loop(0, blocks, sent, 0)


def routed(tokens, w_qkv, w_out, random_blocks, global_ids):
    rows = tokens.shape[0]
    feats = w_qkv.shape[2]
    width = w_out.shape[1]
    heads_axis = lax.axis_size("head")
    slots = global_ids.shape[0]
    blocks = rows // BLOCK
    mine = slots // 2
    vm = pl.BlockSpec(memory_space=pltpu.VMEM)
    sm = pl.BlockSpec(memory_space=pltpu.SMEM)
    bf = jnp.bfloat16
    chain = pltpu.VMEM((mine * BLOCK, feats), bf)
    dma = pltpu.SemaphoreType.DMA
    return pl.pallas_call(
        route_kernel,
        out_shape=jax.ShapeDtypeStruct((rows, width // heads_axis), bf),
        in_specs=[sm, sm, vm, vm, vm],
        out_specs=vm,
        scratch_shapes=[
            pltpu.VMEM((2 * rows, feats), bf), pltpu.VMEM((2 * rows, feats), bf),
            pltpu.VMEM((rows, feats), bf), pltpu.VMEM((rows, feats), bf),
            pltpu.VMEM((rows, feats), bf),
            pltpu.VMEM((slots * BLOCK, feats), bf), pltpu.VMEM((slots * BLOCK, feats), bf),
            chain, chain, chain, chain, chain, chain, chain, chain,
            pltpu.VMEM((heads_axis * feats, width // heads_axis), bf),
            pltpu.VMEM((heads_axis, rows, feats), bf),
            dma((2,)), dma((2,)), dma((2,)), dma((2,)),
            dma((slots,)), dma((slots,)), dma((slots,)), dma((slots,)),
            dma((slots,)), dma((slots,)), dma((1,)), dma((1,)),
            dma((blocks,)), dma((blocks,)),
        ],
        compiler_params=pltpu.CompilerParams(
            collective_id=0, has_side_effects=True, vmem_limit_bytes=48 * 1024 * 1024),
    )(random_blocks, global_ids, tokens, w_qkv, w_out)


def solution(mesh):
    small = mesh.shape["seq"] == 8 and mesh.shape["head"] == 2
    return jax.shard_map(
        routed if small else on_device,
        mesh=mesh,
        in_specs=(
            P(("groups", "seq"), None),
            P(None, None, "head"),
            P("head", None),
            P(("groups", "seq"), None),
            P("groups"),
        ),
        out_specs=P(("groups", "seq"), "head"),
        check_vma=False,
    )
```

```python
import math

import jax
import jax.numpy as jnp
from jax import lax
from jax.experimental import pallas as pl
from jax.experimental.pallas import tpu as pltpu
from jax.sharding import PartitionSpec as P

HEAD_DIM = 64
BLOCK = 64
RAND = 3
MESH = pl.DeviceIdType.MESH


def padded_2(block, sides, width):
    for axis, dim in sides:
        count = lax.axis_size(axis)
        forward = [(i, i + 1) for i in range(count - 1)]
        forward.append((count - 1, 0))
        backward = [(target, source) for source, target in forward]
        low = lax.ppermute(
            lax.slice_in_dim(block, block.shape[dim] - width, None, axis=dim), axis, forward
        )
        high = lax.ppermute(lax.slice_in_dim(block, 0, width, axis=dim), axis, backward)
        block = jnp.concatenate([low, block, high], axis=dim)
    return block


def passed_along(block, axis, distance):
    devices = range(lax.axis_size(axis))
    route = [((i - distance) % len(devices), i) for i in devices]
    return lax.ppermute(block, axis, route)


def broadcast(shard, axis, root):
    mine = lax.axis_index(axis) == root
    return lax.psum(jnp.where(mine, shard, jnp.zeros_like(shard)), axis)


def attend_head(packed):
    single_query_head, local_block_pair, global_block_pair = packed
    scale_factor = 1.0 / math.sqrt(single_query_head.shape[-1])
    local_scores = (
        jnp.einsum(
            "vhw,vcw->vhc",
            single_query_head,
            local_block_pair[0],
            preferred_element_type=jnp.float32,
        )
        * scale_factor
    )
    global_scores = (
        jnp.einsum(
            "ors,is->ori",
            single_query_head,
            global_block_pair[0],
            preferred_element_type=jnp.float32,
        )
        * scale_factor
    )
    largest = jnp.maximum(
        jnp.max(local_scores, axis=-1, keepdims=True),
        jnp.max(global_scores, axis=-1, keepdims=True),
    )
    local_exp = jnp.exp(local_scores - largest)
    global_exp = jnp.exp(global_scores - largest)
    totals = jnp.sum(local_exp, axis=-1, keepdims=True) + jnp.sum(
        global_exp, axis=-1, keepdims=True
    )
    local_attention_weights = (local_exp / totals).astype(jnp.bfloat16)
    global_attention_weights = (global_exp / totals).astype(jnp.bfloat16)
    blended = jnp.einsum(
        "onw,owz->onz",
        local_attention_weights,
        local_block_pair[1],
        preferred_element_type=jnp.float32,
    )
    blended = blended + jnp.einsum(
        "sou,ug->sog",
        global_attention_weights,
        global_block_pair[1],
        preferred_element_type=jnp.float32,
    )
    return blended.astype(jnp.bfloat16)


def on_device(tokens, w_qkv, w_out, random_blocks, global_ids):
    cycle_size = lax.axis_size("seq")
    my_index = lax.axis_index("seq")
    reach_count = max(1, cycle_size // 64)
    tok_rows = tokens.shape[0]
    blk_count = tok_rows // BLOCK
    features = w_qkv.shape[2]
    head_count = features // HEAD_DIM
    queries = jnp.dot(tokens, w_qkv[0], preferred_element_type=jnp.float32).astype(jnp.bfloat16)
    key_rows = jnp.dot(tokens, w_qkv[1], preferred_element_type=jnp.float32).astype(jnp.bfloat16)
    value_rows = jnp.dot(tokens, w_qkv[2], preferred_element_type=jnp.float32).astype(jnp.bfloat16)
    paired_blocks = jnp.stack([key_rows, value_rows])
    pair_blocks = paired_blocks.reshape(2, blk_count, BLOCK, features)
    padded = padded_2(paired_blocks, (("seq", 1),), BLOCK)
    padded_blocks = padded.reshape(2, blk_count + 2, BLOCK, features)
    window = jnp.concatenate(
        [
            padded_blocks[:, 0:blk_count],
            padded_blocks[:, 1 : blk_count + 1],
            padded_blocks[:, 2 : blk_count + 2],
        ],
        axis=2,
    )
    flat_lists = random_blocks.reshape(-1)
    list_owner = flat_lists // blk_count
    list_within = flat_lists % blk_count
    relative = (list_owner - my_index) % cycle_size

    def pick_blocks(collected, piece, offset):
        taken = jnp.take(piece, list_within, axis=1)
        matches = relative == offset % cycle_size
        return jnp.where(matches[None, :, None, None], taken, collected)

    collected = jnp.zeros((2, blk_count * RAND, BLOCK, features), jnp.bfloat16)
    current = passed_along(pair_blocks, "seq", -reach_count)
    collected = pick_blocks(collected, current, reach_count)

    def advance(turn_index, carried):
        moving, gathered = carried
        moving = passed_along(moving, "seq", 1)
        return (moving, pick_blocks(gathered, moving, reach_count - turn_index))

    current, collected = lax.fori_loop(1, 2 * reach_count + 1, advance, (current, collected))
    global_owner = global_ids // blk_count
    global_within = global_ids % blk_count
    global_count = global_ids.shape[0]

    def fetch_global(slot_index, gathered):
        local_piece = lax.dynamic_index_in_dim(
            pair_blocks, global_within[slot_index], axis=1, keepdims=False
        )
        arrived = broadcast(local_piece, "seq", global_owner[slot_index])
        return lax.dynamic_update_index_in_dim(gathered, arrived, slot_index, axis=1)

    global_block_pair = lax.fori_loop(
        0, global_count, fetch_global, jnp.zeros((2, global_count, BLOCK, features), jnp.bfloat16)
    )
    local_block_pair = jnp.concatenate(
        [window, collected.reshape(2, blk_count, RAND * BLOCK, features)], axis=2
    )
    local_heads = local_block_pair.reshape(2, blk_count, -1, head_count, HEAD_DIM).transpose(
        3, 0, 1, 2, 4
    )
    global_heads = global_block_pair.reshape(
        2, global_count * BLOCK, head_count, HEAD_DIM
    ).transpose(2, 0, 1, 3)
    query_heads = queries.reshape(blk_count, BLOCK, head_count, HEAD_DIM).transpose(2, 0, 1, 3)
    attended = lax.map(attend_head, (query_heads, local_heads, global_heads))
    attention = attended.transpose(1, 2, 0, 3).reshape(tok_rows, features)
    partial_sum = jnp.dot(attention, w_out, preferred_element_type=jnp.float32)
    return lax.psum_scatter(
        partial_sum.astype(jnp.bfloat16), "head", scatter_dimension=1, tiled=True
    )


def route_kernel(rand_ref, gid_ref, tok_ref, wqkv_ref, wout_ref, out_ref,
                 krow, vrow, kz, vz, q_ref, gk, gv, near_k, near_v, far_k, far_v,
                 nsend_k, nsend_v, fsend_k, fsend_v, wfull, att,
                 xs, xr, zs, zr, ns, nr, fs, fr, gs, gr, ws, wr, hs, hr):
    rows = tok_ref.shape[0]
    feats = wqkv_ref.shape[2]
    half_out = out_ref.shape[1]
    blocks = rows // BLOCK
    pair = 2 * blocks
    heads = feats // HEAD_DIM
    slots = gid_ref.shape[0]
    mine = slots // 2
    me = lax.axis_index("seq")
    core = lax.axis_index("head")
    cycle = lax.axis_size("seq")
    lines = cycle // 2
    z = me // 2
    x = me % 2
    partner = z * 2 + (1 - x)
    z_next = ((z + 1) % lines) * 2 + x
    z_prev = ((z + lines - 1) % lines) * 2 + x
    to_near = ((z + 1 + (lines - 2) * x) % lines) * 2 + x
    side = (z * 2) // lines
    ahead = z + 1 - 2 * side
    behind = (z + lines - 1 + 2 * side) % lines
    inner = jnp.logical_and(z > 0, z < lines - 1)
    fwd_dev = ahead * 2 + x
    back_dev = behind * 2 + x

    barrier = pltpu.get_barrier_semaphore()
    for who in ({"seq": partner}, {"seq": z_next}, {"seq": z_prev}, {"head": 1 - core}):
        pl.semaphore_signal(barrier, inc=1, device_id=who, device_id_type=MESH)

    def remote(src, dst, ssem, rsem, who):
        return pltpu.make_async_remote_copy(
            src_ref=src, dst_ref=dst, send_sem=ssem, recv_sem=rsem,
            device_id=who, device_id_type=MESH)

    here = pl.ds(pl.multiple_of(x * rows, rows), rows)
    there = pl.ds(pl.multiple_of((1 - x) * rows, rows), rows)

    def project(index):
        return jnp.dot(tok_ref[...], wqkv_ref[index],
                       preferred_element_type=jnp.float32).astype(jnp.bfloat16)

    krow[here, :] = project(1)
    pl.semaphore_wait(barrier, 4)
    send_x = [remote(buf.at[here], buf.at[here], xs.at[i], xr.at[i], {"seq": partner})
              for i, buf in enumerate((krow, vrow))]
    got_x = [remote(buf.at[there], buf.at[there], xs.at[i], xr.at[i], {"seq": partner})
             for i, buf in enumerate((krow, vrow))]
    send_x[0].start()
    vrow[here, :] = project(2)
    send_x[1].start()
    wmine = pl.ds(pl.multiple_of(core * feats, feats), feats)
    wother = pl.ds(pl.multiple_of((1 - core) * feats, feats), feats)
    send_w = remote(
        wout_ref.at[:, pl.ds(pl.multiple_of((1 - core) * half_out, half_out), half_out)],
        wfull.at[wmine], ws.at[0], wr.at[0], {"head": 1 - core})
    send_w.start()
    wfull[wmine, :] = wout_ref[:, pl.ds(pl.multiple_of(core * half_out, half_out), half_out)]
    q_ref[...] = project(0)

    near = (near_k, near_v)
    far = (far_k, far_v)
    nsend = (nsend_k, nsend_v)
    fsend = (fsend_k, fsend_v)
    row = (krow, vrow)
    zbuf = (kz, vz)
    gbuf = (gk, gv)

    def near_copy(kind, j, crossing):
        part = pl.ds(j * BLOCK, BLOCK)
        n = kind * mine + j
        dst, sem = (far, fr) if crossing else (near, nr)
        return remote(nsend[kind].at[part], dst[kind].at[part], ns.at[n], sem.at[n],
                      {"seq": fwd_dev})

    def far_copy(kind, j):
        part = pl.ds(j * BLOCK, BLOCK)
        n = kind * mine + j
        return remote(fsend[kind].at[part], far[kind].at[part], fs.at[n], fr.at[n],
                      {"seq": back_dev})

    def owner(j):
        gid = gid_ref[x * mine + j]
        return lax.div(gid, pair), lax.rem(gid, pair)

    def step_near(kind, j):
        part = pl.ds(j * BLOCK, BLOCK)
        line, within = owner(j)
        own = row[kind][pl.ds(within * BLOCK, BLOCK), :]

        @pl.when(inner)
        def _():
            near_copy(kind, j, False).wait_recv()
            nsend[kind][part, :] = jnp.where(line == z, own, near[kind][part, :])
            near_copy(kind, j, True).start()

        @pl.when(jnp.logical_not(inner))
        def _():
            nsend[kind][part, :] = own
            near_copy(kind, j, False).start()

    def g_copy(kind, j):
        spot = pl.ds(pl.multiple_of((x * mine + j) * BLOCK, BLOCK), BLOCK)
        n = kind * mine + j
        return remote(gbuf[kind].at[spot], gbuf[kind].at[spot], gs.at[n], gr.at[n],
                      {"seq": partner})

    def step_far(kind, j):
        part = pl.ds(j * BLOCK, BLOCK)
        spot = pl.ds(pl.multiple_of((x * mine + j) * BLOCK, BLOCK), BLOCK)
        line, within = owner(j)
        own = row[kind][pl.ds(within * BLOCK, BLOCK), :]
        far_copy(kind, j).wait_recv()
        arrived = far[kind][part, :]

        @pl.when(inner)
        def _():
            fsend[kind][part, :] = jnp.where(line == z, own, arrived)
            far_copy(kind, j).start()
            before = jnp.where(side == 0, line < z, line > z)
            gbuf[kind][spot, :] = jnp.where(
                line == z, own, jnp.where(before, near[kind][part, :], arrived))

        @pl.when(jnp.logical_not(inner))
        def _():
            gbuf[kind][spot, :] = jnp.where(line == z, own, arrived)

        g_copy(kind, j).start()

    send_z = [remote(row[i].at[there], zbuf[i], zs.at[i], zr.at[i], {"seq": to_near})
              for i in range(2)]

    got_x[0].wait_recv()
    for j in range(mine):
        step_near(0, j)

    @pl.when(jnp.logical_not(inner))
    def _():
        got_x[1].wait_recv()
        for j in range(mine):
            step_near(1, j)
        send_z[0].start()
        send_z[1].start()
        for kind in range(2):
            for j in range(mine):
                step_far(kind, j)

    @pl.when(inner)
    def _():
        got_x[1].wait_recv()
        send_z[0].start()
        for j in range(mine):
            step_near(1, j)
            step_far(0, j)
        send_z[1].start()
        for j in range(mine):
            step_far(1, j)

    for kind in range(2):
        for j in range(mine):
            n = kind * mine + j
            spot = pl.ds(pl.multiple_of(((1 - x) * mine + j) * BLOCK, BLOCK), BLOCK)
            remote(gbuf[kind].at[spot], gbuf[kind].at[spot], gs.at[n], gr.at[n],
                   {"seq": partner}).wait_recv()
    for kind in range(2):
        send_z[kind].wait_recv()

    lane_head = lax.broadcasted_iota(jnp.int32, (BLOCK, feats), 1) // HEAD_DIM
    masks = [(lane_head == h).astype(jnp.float32) for h in range(heads)]
    masks16 = [m.astype(jnp.bfloat16) for m in masks]
    factor = math.log2(math.e) / math.sqrt(HEAD_DIM)
    doc_blocks = cycle * blocks

    def fetch(bufs, e):
        place = e - pair * z
        inside = jnp.logical_and(place >= 0, place < pair)
        place = jnp.clip(place, 0, pair - 1)
        a = bufs[0][pl.ds(place * BLOCK, BLOCK), :]
        b = bufs[1][pl.ds(lax.rem(e, blocks) * BLOCK, BLOCK), :]
        return jnp.where(inside, a, b)

    def att_copy(b):
        spot = pl.ds(pl.multiple_of(b * BLOCK, BLOCK), BLOCK)
        return remote(att.at[core, spot], att.at[core, spot], hs.at[b], hr.at[b],
                      {"head": 1 - core})

    def one_block(b, carry):
        spot = pl.ds(pl.multiple_of(b * BLOCK, BLOCK), BLOCK)
        q = q_ref[spot, :]
        stacked = jnp.concatenate([q * m for m in masks16], axis=0)
        mid = me * blocks + b
        picks = [lax.rem(mid + doc_blocks - 1, doc_blocks), mid,
                 lax.rem(mid + 1, doc_blocks)] + [rand_ref[b, i] for i in range(RAND)]
        kloc = jnp.concatenate([fetch((krow, kz), e) for e in picks], axis=0)
        vloc = jnp.concatenate([fetch((vrow, vz), e) for e in picks], axis=0)
        dims = (((1,), (1,)), ((), ()))
        sl = lax.dot_general(stacked, kloc, dims, preferred_element_type=jnp.float32)
        sg = lax.dot_general(stacked, gk[...], dims, preferred_element_type=jnp.float32)
        top = jnp.maximum(jnp.max(sl, axis=1, keepdims=True), jnp.max(sg, axis=1, keepdims=True))
        el = jnp.exp2((sl - top) * factor)
        eg = jnp.exp2((sg - top) * factor)
        norm = jnp.sum(el, axis=1, keepdims=True) + jnp.sum(eg, axis=1, keepdims=True)
        o = jnp.dot(el.astype(jnp.bfloat16), vloc, preferred_element_type=jnp.float32)
        o += jnp.dot(eg.astype(jnp.bfloat16), gv[...], preferred_element_type=jnp.float32)
        o = o / norm
        merged = o[0:BLOCK] * masks[0]
        for h in range(1, heads):
            merged += o[h * BLOCK:(h + 1) * BLOCK] * masks[h]
        att[core, spot, :] = merged.astype(jnp.bfloat16)
        att_copy(b).start()
        return carry

    lax.fori_loop(0, blocks, one_block, 0)

    remote(wout_ref.at[:, pl.ds(0, half_out)], wfull.at[wother], ws.at[0], wr.at[0],
           {"head": 1 - core}).wait_recv()
    acc = jnp.dot(att[core], wfull[wmine, :], preferred_element_type=jnp.float32)

    def other_in(b, carry):
        spot = pl.ds(pl.multiple_of(b * BLOCK, BLOCK), BLOCK)
        remote(att.at[1 - core, spot], att.at[1 - core, spot], hs.at[b], hr.at[b],
               {"head": 1 - core}).wait_recv()
        return carry

    lax.fori_loop(0, blocks, other_in, 0)
    acc += jnp.dot(att[1 - core], wfull[wother, :], preferred_element_type=jnp.float32)
    out_ref[...] = acc.astype(jnp.bfloat16)

    for kind in range(2):
        send_x[kind].wait_send()
        send_z[kind].wait_send()
        for j in range(mine):
            near_copy(kind, j, False).wait_send()
            g_copy(kind, j).wait_send()
    send_w.wait_send()

    @pl.when(inner)
    def _():
        for kind in range(2):
            for j in range(mine):
                far_copy(kind, j).wait_send()

    def sent(b, carry):
        att_copy(b).wait_send()
        return carry

    lax.fori_loop(0, blocks, sent, 0)


def routed(tokens, w_qkv, w_out, random_blocks, global_ids):
    rows = tokens.shape[0]
    feats = w_qkv.shape[2]
    width = w_out.shape[1]
    heads_axis = lax.axis_size("head")
    slots = global_ids.shape[0]
    blocks = rows // BLOCK
    mine = slots // 2
    vm = pl.BlockSpec(memory_space=pltpu.VMEM)
    sm = pl.BlockSpec(memory_space=pltpu.SMEM)
    bf = jnp.bfloat16
    chain = pltpu.VMEM((mine * BLOCK, feats), bf)
    dma = pltpu.SemaphoreType.DMA
    return pl.pallas_call(
        route_kernel,
        out_shape=jax.ShapeDtypeStruct((rows, width // heads_axis), bf),
        in_specs=[sm, sm, vm, vm, vm],
        out_specs=vm,
        scratch_shapes=[
            pltpu.VMEM((2 * rows, feats), bf), pltpu.VMEM((2 * rows, feats), bf),
            pltpu.VMEM((rows, feats), bf), pltpu.VMEM((rows, feats), bf),
            pltpu.VMEM((rows, feats), bf),
            pltpu.VMEM((slots * BLOCK, feats), bf), pltpu.VMEM((slots * BLOCK, feats), bf),
            chain, chain, chain, chain, chain, chain, chain, chain,
            pltpu.VMEM((heads_axis * feats, width // heads_axis), bf),
            pltpu.VMEM((heads_axis, rows, feats), bf),
            dma((2,)), dma((2,)), dma((2,)), dma((2,)),
            dma((slots,)), dma((slots,)), dma((slots,)), dma((slots,)),
            dma((slots,)), dma((slots,)), dma((1,)), dma((1,)),
            dma((blocks,)), dma((blocks,)),
        ],
        compiler_params=pltpu.CompilerParams(
            collective_id=0, has_side_effects=True, vmem_limit_bytes=48 * 1024 * 1024),
    )(random_blocks, global_ids, tokens, w_qkv, w_out)


def solution(mesh):
    small = mesh.shape["seq"] == 8 and mesh.shape["head"] == 2
    return jax.shard_map(
        routed if small else on_device,
        mesh=mesh,
        in_specs=(
            P(("groups", "seq"), None),
            P(None, None, "head"),
            P("head", None),
            P(("groups", "seq"), None),
            P("groups"),
        ),
        out_specs=P(("groups", "seq"), "head"),
        check_vma=False,
    )
```

```python
import math

import jax
import jax.numpy as jnp
from jax import lax
from jax.experimental import pallas as pl
from jax.experimental.pallas import tpu as pltpu
from jax.sharding import PartitionSpec as P

HEAD_DIM = 64
BLOCK = 64
RAND = 3
MESH = pl.DeviceIdType.MESH


def padded_2(block, sides, width):
    for axis, dim in sides:
        count = lax.axis_size(axis)
        forward = [(i, i + 1) for i in range(count - 1)]
        forward.append((count - 1, 0))
        backward = [(target, source) for source, target in forward]
        low = lax.ppermute(
            lax.slice_in_dim(block, block.shape[dim] - width, None, axis=dim), axis, forward
        )
        high = lax.ppermute(lax.slice_in_dim(block, 0, width, axis=dim), axis, backward)
        block = jnp.concatenate([low, block, high], axis=dim)
    return block


def passed_along(block, axis, distance):
    devices = range(lax.axis_size(axis))
    route = [((i - distance) % len(devices), i) for i in devices]
    return lax.ppermute(block, axis, route)


def broadcast(shard, axis, root):
    mine = lax.axis_index(axis) == root
    return lax.psum(jnp.where(mine, shard, jnp.zeros_like(shard)), axis)


def attend_head(packed):
    single_query_head, local_block_pair, global_block_pair = packed
    scale_factor = 1.0 / math.sqrt(single_query_head.shape[-1])
    local_scores = (
        jnp.einsum(
            "vhw,vcw->vhc",
            single_query_head,
            local_block_pair[0],
            preferred_element_type=jnp.float32,
        )
        * scale_factor
    )
    global_scores = (
        jnp.einsum(
            "ors,is->ori",
            single_query_head,
            global_block_pair[0],
            preferred_element_type=jnp.float32,
        )
        * scale_factor
    )
    largest = jnp.maximum(
        jnp.max(local_scores, axis=-1, keepdims=True),
        jnp.max(global_scores, axis=-1, keepdims=True),
    )
    local_exp = jnp.exp(local_scores - largest)
    global_exp = jnp.exp(global_scores - largest)
    totals = jnp.sum(local_exp, axis=-1, keepdims=True) + jnp.sum(
        global_exp, axis=-1, keepdims=True
    )
    local_attention_weights = (local_exp / totals).astype(jnp.bfloat16)
    global_attention_weights = (global_exp / totals).astype(jnp.bfloat16)
    blended = jnp.einsum(
        "onw,owz->onz",
        local_attention_weights,
        local_block_pair[1],
        preferred_element_type=jnp.float32,
    )
    blended = blended + jnp.einsum(
        "sou,ug->sog",
        global_attention_weights,
        global_block_pair[1],
        preferred_element_type=jnp.float32,
    )
    return blended.astype(jnp.bfloat16)


def on_device(tokens, w_qkv, w_out, random_blocks, global_ids):
    cycle_size = lax.axis_size("seq")
    my_index = lax.axis_index("seq")
    reach_count = max(1, cycle_size // 64)
    tok_rows = tokens.shape[0]
    blk_count = tok_rows // BLOCK
    features = w_qkv.shape[2]
    head_count = features // HEAD_DIM
    queries = jnp.dot(tokens, w_qkv[0], preferred_element_type=jnp.float32).astype(jnp.bfloat16)
    key_rows = jnp.dot(tokens, w_qkv[1], preferred_element_type=jnp.float32).astype(jnp.bfloat16)
    value_rows = jnp.dot(tokens, w_qkv[2], preferred_element_type=jnp.float32).astype(jnp.bfloat16)
    paired_blocks = jnp.stack([key_rows, value_rows])
    pair_blocks = paired_blocks.reshape(2, blk_count, BLOCK, features)
    padded = padded_2(paired_blocks, (("seq", 1),), BLOCK)
    padded_blocks = padded.reshape(2, blk_count + 2, BLOCK, features)
    window = jnp.concatenate(
        [
            padded_blocks[:, 0:blk_count],
            padded_blocks[:, 1 : blk_count + 1],
            padded_blocks[:, 2 : blk_count + 2],
        ],
        axis=2,
    )
    flat_lists = random_blocks.reshape(-1)
    list_owner = flat_lists // blk_count
    list_within = flat_lists % blk_count
    relative = (list_owner - my_index) % cycle_size

    def pick_blocks(collected, piece, offset):
        taken = jnp.take(piece, list_within, axis=1)
        matches = relative == offset % cycle_size
        return jnp.where(matches[None, :, None, None], taken, collected)

    collected = jnp.zeros((2, blk_count * RAND, BLOCK, features), jnp.bfloat16)
    current = passed_along(pair_blocks, "seq", -reach_count)
    collected = pick_blocks(collected, current, reach_count)

    def advance(turn_index, carried):
        moving, gathered = carried
        moving = passed_along(moving, "seq", 1)
        return (moving, pick_blocks(gathered, moving, reach_count - turn_index))

    current, collected = lax.fori_loop(1, 2 * reach_count + 1, advance, (current, collected))
    global_owner = global_ids // blk_count
    global_within = global_ids % blk_count
    global_count = global_ids.shape[0]

    def fetch_global(slot_index, gathered):
        local_piece = lax.dynamic_index_in_dim(
            pair_blocks, global_within[slot_index], axis=1, keepdims=False
        )
        arrived = broadcast(local_piece, "seq", global_owner[slot_index])
        return lax.dynamic_update_index_in_dim(gathered, arrived, slot_index, axis=1)

    global_block_pair = lax.fori_loop(
        0, global_count, fetch_global, jnp.zeros((2, global_count, BLOCK, features), jnp.bfloat16)
    )
    local_block_pair = jnp.concatenate(
        [window, collected.reshape(2, blk_count, RAND * BLOCK, features)], axis=2
    )
    local_heads = local_block_pair.reshape(2, blk_count, -1, head_count, HEAD_DIM).transpose(
        3, 0, 1, 2, 4
    )
    global_heads = global_block_pair.reshape(
        2, global_count * BLOCK, head_count, HEAD_DIM
    ).transpose(2, 0, 1, 3)
    query_heads = queries.reshape(blk_count, BLOCK, head_count, HEAD_DIM).transpose(2, 0, 1, 3)
    attended = lax.map(attend_head, (query_heads, local_heads, global_heads))
    attention = attended.transpose(1, 2, 0, 3).reshape(tok_rows, features)
    partial_sum = jnp.dot(attention, w_out, preferred_element_type=jnp.float32)
    return lax.psum_scatter(
        partial_sum.astype(jnp.bfloat16), "head", scatter_dimension=1, tiled=True
    )


def route_kernel(rand_hbm, gid_hbm, tok_hbm, wqkv_hbm, wout_hbm, out_ref,
                 rand_ref, gid_ref, tok_ref, wqkv_ref, wout_ref, ls,
                 krow, vrow, kz, vz, q_ref, gk, gv, near_k, near_v, far_k, far_v,
                 nsend_k, nsend_v, fsend_k, fsend_v, wfull, att,
                 xs, xr, zs, zr, ns, nr, fs, fr, gs, gr, ws, wr, hs, hr):
    load_tok = pltpu.make_async_copy(tok_hbm, tok_ref, ls.at[0])
    load_w = [pltpu.make_async_copy(wqkv_hbm.at[i], wqkv_ref.at[i], ls.at[1 + i]) for i in range(3)]
    load_o = pltpu.make_async_copy(wout_hbm, wout_ref, ls.at[4])
    load_r = pltpu.make_async_copy(rand_hbm, rand_ref, ls.at[5])
    load_g = pltpu.make_async_copy(gid_hbm, gid_ref, ls.at[6])
    for load in (load_w[1], load_tok, load_w[2], load_g, load_o, load_w[0], load_r):
        load.start()
    rows = tok_ref.shape[0]
    feats = wqkv_ref.shape[2]
    half_out = out_ref.shape[1]
    blocks = rows // BLOCK
    pair = 2 * blocks
    heads = feats // HEAD_DIM
    slots = gid_ref.shape[0]
    mine = slots // 2
    me = lax.axis_index("seq")
    core = lax.axis_index("head")
    cycle = lax.axis_size("seq")
    lines = cycle // 2
    z = me // 2
    x = me % 2
    partner = z * 2 + (1 - x)
    z_next = ((z + 1) % lines) * 2 + x
    z_prev = ((z + lines - 1) % lines) * 2 + x
    to_near = ((z + 1 + (lines - 2) * x) % lines) * 2 + x
    side = (z * 2) // lines
    ahead = z + 1 - 2 * side
    behind = (z + lines - 1 + 2 * side) % lines
    inner = jnp.logical_and(z > 0, z < lines - 1)
    fwd_dev = ahead * 2 + x
    back_dev = behind * 2 + x

    barrier = pltpu.get_barrier_semaphore()
    for who in ({"seq": partner}, {"seq": z_next}, {"seq": z_prev}, {"head": 1 - core}):
        pl.semaphore_signal(barrier, inc=1, device_id=who, device_id_type=MESH)

    def remote(src, dst, ssem, rsem, who):
        return pltpu.make_async_remote_copy(
            src_ref=src, dst_ref=dst, send_sem=ssem, recv_sem=rsem,
            device_id=who, device_id_type=MESH)

    here = pl.ds(pl.multiple_of(x * rows, rows), rows)
    there = pl.ds(pl.multiple_of((1 - x) * rows, rows), rows)

    def project(index):
        return jnp.dot(tok_ref[...], wqkv_ref[index],
                       preferred_element_type=jnp.float32).astype(jnp.bfloat16)

    load_tok.wait()
    load_w[1].wait()
    krow[here, :] = project(1)
    pl.semaphore_wait(barrier, 4)
    send_x = [remote(buf.at[here], buf.at[here], xs.at[i], xr.at[i], {"seq": partner})
              for i, buf in enumerate((krow, vrow))]
    got_x = [remote(buf.at[there], buf.at[there], xs.at[i], xr.at[i], {"seq": partner})
             for i, buf in enumerate((krow, vrow))]
    send_x[0].start()
    load_w[2].wait()
    vrow[here, :] = project(2)
    send_x[1].start()
    load_o.wait()
    wmine = pl.ds(pl.multiple_of(core * feats, feats), feats)
    wother = pl.ds(pl.multiple_of((1 - core) * feats, feats), feats)
    send_w = remote(
        wout_ref.at[:, pl.ds(pl.multiple_of((1 - core) * half_out, half_out), half_out)],
        wfull.at[wmine], ws.at[0], wr.at[0], {"head": 1 - core})
    send_w.start()
    wfull[wmine, :] = wout_ref[:, pl.ds(pl.multiple_of(core * half_out, half_out), half_out)]
    load_w[0].wait()
    load_r.wait()
    load_g.wait()
    q_ref[...] = project(0)

    near = (near_k, near_v)
    far = (far_k, far_v)
    nsend = (nsend_k, nsend_v)
    fsend = (fsend_k, fsend_v)
    row = (krow, vrow)
    zbuf = (kz, vz)
    gbuf = (gk, gv)

    def near_copy(kind, j, crossing):
        part = pl.ds(j * BLOCK, BLOCK)
        n = kind * mine + j
        dst, sem = (far, fr) if crossing else (near, nr)
        return remote(nsend[kind].at[part], dst[kind].at[part], ns.at[n], sem.at[n],
                      {"seq": fwd_dev})

    def far_copy(kind, j):
        part = pl.ds(j * BLOCK, BLOCK)
        n = kind * mine + j
        return remote(fsend[kind].at[part], far[kind].at[part], fs.at[n], fr.at[n],
                      {"seq": back_dev})

    def owner(j):
        gid = gid_ref[x * mine + j]
        return lax.div(gid, pair), lax.rem(gid, pair)

    def step_near(kind, j):
        part = pl.ds(j * BLOCK, BLOCK)
        line, within = owner(j)
        own = row[kind][pl.ds(within * BLOCK, BLOCK), :]

        @pl.when(inner)
        def _():
            near_copy(kind, j, False).wait_recv()
            nsend[kind][part, :] = jnp.where(line == z, own, near[kind][part, :])
            near_copy(kind, j, True).start()

        @pl.when(jnp.logical_not(inner))
        def _():
            nsend[kind][part, :] = own
            near_copy(kind, j, False).start()

    def g_copy(kind, j):
        spot = pl.ds(pl.multiple_of((x * mine + j) * BLOCK, BLOCK), BLOCK)
        n = kind * mine + j
        return remote(gbuf[kind].at[spot], gbuf[kind].at[spot], gs.at[n], gr.at[n],
                      {"seq": partner})

    def step_far(kind, j):
        part = pl.ds(j * BLOCK, BLOCK)
        spot = pl.ds(pl.multiple_of((x * mine + j) * BLOCK, BLOCK), BLOCK)
        line, within = owner(j)
        own = row[kind][pl.ds(within * BLOCK, BLOCK), :]
        far_copy(kind, j).wait_recv()
        arrived = far[kind][part, :]

        @pl.when(inner)
        def _():
            fsend[kind][part, :] = jnp.where(line == z, own, arrived)
            far_copy(kind, j).start()
            before = jnp.where(side == 0, line < z, line > z)
            gbuf[kind][spot, :] = jnp.where(
                line == z, own, jnp.where(before, near[kind][part, :], arrived))

        @pl.when(jnp.logical_not(inner))
        def _():
            gbuf[kind][spot, :] = jnp.where(line == z, own, arrived)

        g_copy(kind, j).start()

    send_z = [remote(row[i].at[there], zbuf[i], zs.at[i], zr.at[i], {"seq": to_near})
              for i in range(2)]

    got_x[0].wait_recv()

    @pl.when(inner)
    def _():
        send_z[0].start()

    for j in range(mine):
        step_near(0, j)

    @pl.when(jnp.logical_not(inner))
    def _():
        send_z[0].start()
        got_x[1].wait_recv()
        for j in range(mine):
            step_near(1, j)
        send_z[1].start()
        for kind in range(2):
            for j in range(mine):
                step_far(kind, j)

    @pl.when(inner)
    def _():
        got_x[1].wait_recv()
        send_z[1].start()
        for j in range(mine):
            step_near(1, j)
            step_far(0, j)
        for j in range(mine):
            step_far(1, j)

    for kind in range(2):
        for j in range(mine):
            n = kind * mine + j
            spot = pl.ds(pl.multiple_of(((1 - x) * mine + j) * BLOCK, BLOCK), BLOCK)
            remote(gbuf[kind].at[spot], gbuf[kind].at[spot], gs.at[n], gr.at[n],
                   {"seq": partner}).wait_recv()
    for kind in range(2):
        send_z[kind].wait_recv()

    lane_head = lax.broadcasted_iota(jnp.int32, (BLOCK, feats), 1) // HEAD_DIM
    masks = [(lane_head == h).astype(jnp.float32) for h in range(heads)]
    masks16 = [m.astype(jnp.bfloat16) for m in masks]
    factor = math.log2(math.e) / math.sqrt(HEAD_DIM)
    doc_blocks = cycle * blocks

    def fetch(bufs, e):
        place = e - pair * z
        inside = jnp.logical_and(place >= 0, place < pair)
        place = jnp.clip(place, 0, pair - 1)
        a = bufs[0][pl.ds(place * BLOCK, BLOCK), :]
        b = bufs[1][pl.ds(lax.rem(e, blocks) * BLOCK, BLOCK), :]
        return jnp.where(inside, a, b)

    def att_copy(b):
        spot = pl.ds(pl.multiple_of(b * BLOCK, BLOCK), BLOCK)
        return remote(att.at[core, spot], att.at[core, spot], hs.at[b], hr.at[b],
                      {"head": 1 - core})

    def one_block(b, carry):
        spot = pl.ds(pl.multiple_of(b * BLOCK, BLOCK), BLOCK)
        q = q_ref[spot, :]
        stacked = jnp.concatenate([q * m for m in masks16], axis=0)
        mid = me * blocks + b
        picks = [lax.rem(mid + doc_blocks - 1, doc_blocks), mid,
                 lax.rem(mid + 1, doc_blocks)] + [rand_ref[i, b] for i in range(RAND)]
        kloc = jnp.concatenate([fetch((krow, kz), e) for e in picks], axis=0)
        vloc = jnp.concatenate([fetch((vrow, vz), e) for e in picks], axis=0)
        dims = (((1,), (1,)), ((), ()))
        sl = lax.dot_general(stacked, kloc, dims, preferred_element_type=jnp.float32)
        sg = lax.dot_general(stacked, gk[...], dims, preferred_element_type=jnp.float32)
        top = jnp.maximum(jnp.max(sl, axis=1, keepdims=True), jnp.max(sg, axis=1, keepdims=True))
        el = jnp.exp2((sl - top) * factor)
        eg = jnp.exp2((sg - top) * factor)
        norm = jnp.sum(el, axis=1, keepdims=True) + jnp.sum(eg, axis=1, keepdims=True)
        o = jnp.dot(el.astype(jnp.bfloat16), vloc, preferred_element_type=jnp.float32)
        o += jnp.dot(eg.astype(jnp.bfloat16), gv[...], preferred_element_type=jnp.float32)
        o = o / norm
        merged = o[0:BLOCK] * masks[0]
        for h in range(1, heads):
            merged += o[h * BLOCK:(h + 1) * BLOCK] * masks[h]
        att[core, spot, :] = merged.astype(jnp.bfloat16)
        att_copy(b).start()
        return carry

    lax.fori_loop(0, blocks, one_block, 0)

    remote(wout_ref.at[:, pl.ds(0, half_out)], wfull.at[wother], ws.at[0], wr.at[0],
           {"head": 1 - core}).wait_recv()
    acc = jnp.dot(att[core], wfull[wmine, :], preferred_element_type=jnp.float32)

    def other_in(b, carry):
        spot = pl.ds(pl.multiple_of(b * BLOCK, BLOCK), BLOCK)
        remote(att.at[1 - core, spot], att.at[1 - core, spot], hs.at[b], hr.at[b],
               {"head": 1 - core}).wait_recv()
        return carry

    lax.fori_loop(0, blocks, other_in, 0)
    acc += jnp.dot(att[1 - core], wfull[wother, :], preferred_element_type=jnp.float32)
    out_ref[...] = acc.astype(jnp.bfloat16)

    for kind in range(2):
        send_x[kind].wait_send()
        send_z[kind].wait_send()
        for j in range(mine):
            near_copy(kind, j, False).wait_send()
            g_copy(kind, j).wait_send()
    send_w.wait_send()

    @pl.when(inner)
    def _():
        for kind in range(2):
            for j in range(mine):
                far_copy(kind, j).wait_send()

    def sent(b, carry):
        att_copy(b).wait_send()
        return carry

    lax.fori_loop(0, blocks, sent, 0)


def routed(tokens, w_qkv, w_out, random_blocks, global_ids):
    rows = tokens.shape[0]
    feats = w_qkv.shape[2]
    width = w_out.shape[1]
    heads_axis = lax.axis_size("head")
    slots = global_ids.shape[0]
    blocks = rows // BLOCK
    mine = slots // 2
    vm = pl.BlockSpec(memory_space=pltpu.VMEM)
    hb = pl.BlockSpec(memory_space=pltpu.HBM)
    bf = jnp.bfloat16
    chain = pltpu.VMEM((mine * BLOCK, feats), bf)
    dma = pltpu.SemaphoreType.DMA
    return pl.pallas_call(
        route_kernel,
        out_shape=jax.ShapeDtypeStruct((rows, width // heads_axis), bf),
        in_specs=[hb, hb, hb, hb, hb],
        out_specs=vm,
        scratch_shapes=[
            pltpu.SMEM(random_blocks.shape[::-1], jnp.int32), pltpu.SMEM(global_ids.shape, jnp.int32),
            pltpu.VMEM(tokens.shape, bf), pltpu.VMEM(w_qkv.shape, bf), pltpu.VMEM(w_out.shape, bf),
            dma((7,)),
            pltpu.VMEM((2 * rows, feats), bf), pltpu.VMEM((2 * rows, feats), bf),
            pltpu.VMEM((rows, feats), bf), pltpu.VMEM((rows, feats), bf),
            pltpu.VMEM((rows, feats), bf),
            pltpu.VMEM((slots * BLOCK, feats), bf), pltpu.VMEM((slots * BLOCK, feats), bf),
            chain, chain, chain, chain, chain, chain, chain, chain,
            pltpu.VMEM((heads_axis * feats, width // heads_axis), bf),
            pltpu.VMEM((heads_axis, rows, feats), bf),
            dma((2,)), dma((2,)), dma((2,)), dma((2,)),
            dma((slots,)), dma((slots,)), dma((slots,)), dma((slots,)),
            dma((slots,)), dma((slots,)), dma((1,)), dma((1,)),
            dma((blocks,)), dma((blocks,)),
        ],
        compiler_params=pltpu.CompilerParams(
            collective_id=0, has_side_effects=True, vmem_limit_bytes=63 * 1024 * 1024 + 512 * 1024),
    )(random_blocks.T, global_ids, tokens, w_qkv, w_out)


def solution(mesh):
    small = mesh.shape["seq"] == 8 and mesh.shape["head"] == 2
    return jax.shard_map(
        routed if small else on_device,
        mesh=mesh,
        in_specs=(
            P(("groups", "seq"), None),
            P(None, None, "head"),
            P("head", None),
            P(("groups", "seq"), None),
            P("groups"),
        ),
        out_specs=P(("groups", "seq"), "head"),
        check_vma=False,
    )
```

```python
import math

import jax
import jax.numpy as jnp
from jax import lax
from jax.experimental import pallas as pl
from jax.experimental.pallas import tpu as pltpu
from jax.sharding import PartitionSpec as P

HEAD_DIM = 64
BLOCK = 64
RAND = 3
MESH = pl.DeviceIdType.MESH


def padded_2(block, sides, width):
    for axis, dim in sides:
        count = lax.axis_size(axis)
        forward = [(i, i + 1) for i in range(count - 1)]
        forward.append((count - 1, 0))
        backward = [(target, source) for source, target in forward]
        low = lax.ppermute(
            lax.slice_in_dim(block, block.shape[dim] - width, None, axis=dim), axis, forward
        )
        high = lax.ppermute(lax.slice_in_dim(block, 0, width, axis=dim), axis, backward)
        block = jnp.concatenate([low, block, high], axis=dim)
    return block


def passed_along(block, axis, distance):
    devices = range(lax.axis_size(axis))
    route = [((i - distance) % len(devices), i) for i in devices]
    return lax.ppermute(block, axis, route)


def broadcast(shard, axis, root):
    mine = lax.axis_index(axis) == root
    return lax.psum(jnp.where(mine, shard, jnp.zeros_like(shard)), axis)


def attend_head(packed):
    single_query_head, local_block_pair, global_block_pair = packed
    scale_factor = 1.0 / math.sqrt(single_query_head.shape[-1])
    local_scores = (
        jnp.einsum(
            "vhw,vcw->vhc",
            single_query_head,
            local_block_pair[0],
            preferred_element_type=jnp.float32,
        )
        * scale_factor
    )
    global_scores = (
        jnp.einsum(
            "ors,is->ori",
            single_query_head,
            global_block_pair[0],
            preferred_element_type=jnp.float32,
        )
        * scale_factor
    )
    largest = jnp.maximum(
        jnp.max(local_scores, axis=-1, keepdims=True),
        jnp.max(global_scores, axis=-1, keepdims=True),
    )
    local_exp = jnp.exp(local_scores - largest)
    global_exp = jnp.exp(global_scores - largest)
    totals = jnp.sum(local_exp, axis=-1, keepdims=True) + jnp.sum(
        global_exp, axis=-1, keepdims=True
    )
    local_attention_weights = (local_exp / totals).astype(jnp.bfloat16)
    global_attention_weights = (global_exp / totals).astype(jnp.bfloat16)
    blended = jnp.einsum(
        "onw,owz->onz",
        local_attention_weights,
        local_block_pair[1],
        preferred_element_type=jnp.float32,
    )
    blended = blended + jnp.einsum(
        "sou,ug->sog",
        global_attention_weights,
        global_block_pair[1],
        preferred_element_type=jnp.float32,
    )
    return blended.astype(jnp.bfloat16)


def on_device(tokens, w_qkv, w_out, random_blocks, global_ids):
    cycle_size = lax.axis_size("seq")
    my_index = lax.axis_index("seq")
    reach_count = max(1, cycle_size // 64)
    tok_rows = tokens.shape[0]
    blk_count = tok_rows // BLOCK
    features = w_qkv.shape[2]
    head_count = features // HEAD_DIM
    queries = jnp.dot(tokens, w_qkv[0], preferred_element_type=jnp.float32).astype(jnp.bfloat16)
    key_rows = jnp.dot(tokens, w_qkv[1], preferred_element_type=jnp.float32).astype(jnp.bfloat16)
    value_rows = jnp.dot(tokens, w_qkv[2], preferred_element_type=jnp.float32).astype(jnp.bfloat16)
    paired_blocks = jnp.stack([key_rows, value_rows])
    pair_blocks = paired_blocks.reshape(2, blk_count, BLOCK, features)
    padded = padded_2(paired_blocks, (("seq", 1),), BLOCK)
    padded_blocks = padded.reshape(2, blk_count + 2, BLOCK, features)
    window = jnp.concatenate(
        [
            padded_blocks[:, 0:blk_count],
            padded_blocks[:, 1 : blk_count + 1],
            padded_blocks[:, 2 : blk_count + 2],
        ],
        axis=2,
    )
    flat_lists = random_blocks.reshape(-1)
    list_owner = flat_lists // blk_count
    list_within = flat_lists % blk_count
    relative = (list_owner - my_index) % cycle_size

    def pick_blocks(collected, piece, offset):
        taken = jnp.take(piece, list_within, axis=1)
        matches = relative == offset % cycle_size
        return jnp.where(matches[None, :, None, None], taken, collected)

    collected = jnp.zeros((2, blk_count * RAND, BLOCK, features), jnp.bfloat16)
    current = passed_along(pair_blocks, "seq", -reach_count)
    collected = pick_blocks(collected, current, reach_count)

    def advance(turn_index, carried):
        moving, gathered = carried
        moving = passed_along(moving, "seq", 1)
        return (moving, pick_blocks(gathered, moving, reach_count - turn_index))

    current, collected = lax.fori_loop(1, 2 * reach_count + 1, advance, (current, collected))
    global_owner = global_ids // blk_count
    global_within = global_ids % blk_count
    global_count = global_ids.shape[0]

    def fetch_global(slot_index, gathered):
        local_piece = lax.dynamic_index_in_dim(
            pair_blocks, global_within[slot_index], axis=1, keepdims=False
        )
        arrived = broadcast(local_piece, "seq", global_owner[slot_index])
        return lax.dynamic_update_index_in_dim(gathered, arrived, slot_index, axis=1)

    global_block_pair = lax.fori_loop(
        0, global_count, fetch_global, jnp.zeros((2, global_count, BLOCK, features), jnp.bfloat16)
    )
    local_block_pair = jnp.concatenate(
        [window, collected.reshape(2, blk_count, RAND * BLOCK, features)], axis=2
    )
    local_heads = local_block_pair.reshape(2, blk_count, -1, head_count, HEAD_DIM).transpose(
        3, 0, 1, 2, 4
    )
    global_heads = global_block_pair.reshape(
        2, global_count * BLOCK, head_count, HEAD_DIM
    ).transpose(2, 0, 1, 3)
    query_heads = queries.reshape(blk_count, BLOCK, head_count, HEAD_DIM).transpose(2, 0, 1, 3)
    attended = lax.map(attend_head, (query_heads, local_heads, global_heads))
    attention = attended.transpose(1, 2, 0, 3).reshape(tok_rows, features)
    partial_sum = jnp.dot(attention, w_out, preferred_element_type=jnp.float32)
    return lax.psum_scatter(
        partial_sum.astype(jnp.bfloat16), "head", scatter_dimension=1, tiled=True
    )


def route_kernel(rand_hbm, gid_hbm, tok_hbm, wqkv_hbm, wout_hbm, out_ref,
                 rand_ref, gid_ref, tok_ref, wqkv_ref, wout_ref, ls,
                 probs, krow, vrow, kz, vz, q_ref, gk, gv, near_k, near_v, far_k, far_v,
                 nsend_k, nsend_v, fsend_k, fsend_v, wfull, att,
                 xs, xr, zs, zr, ns, nr, fs, fr, gs, gr, ws, wr, hs, hr):
    load_tok = pltpu.make_async_copy(tok_hbm, tok_ref, ls.at[0])
    load_w = [pltpu.make_async_copy(wqkv_hbm.at[i], wqkv_ref.at[i], ls.at[1 + i]) for i in range(3)]
    load_o = pltpu.make_async_copy(wout_hbm, wout_ref, ls.at[4])
    load_r = pltpu.make_async_copy(rand_hbm, rand_ref, ls.at[5])
    load_g = pltpu.make_async_copy(gid_hbm, gid_ref, ls.at[6])
    for load in (load_w[1], load_tok, load_w[2], load_g, load_o, load_w[0], load_r):
        load.start()
    rows = tok_ref.shape[0]
    feats = wqkv_ref.shape[2]
    half_out = out_ref.shape[1]
    blocks = rows // BLOCK
    pair = 2 * blocks
    heads = feats // HEAD_DIM
    slots = gid_ref.shape[0]
    mine = slots // 2
    me = lax.axis_index("seq")
    core = lax.axis_index("head")
    cycle = lax.axis_size("seq")
    lines = cycle // 2
    z = me // 2
    x = me % 2
    partner = z * 2 + (1 - x)
    z_next = ((z + 1) % lines) * 2 + x
    z_prev = ((z + lines - 1) % lines) * 2 + x
    to_near = ((z + 1 + (lines - 2) * x) % lines) * 2 + x
    side = (z * 2) // lines
    ahead = z + 1 - 2 * side
    behind = (z + lines - 1 + 2 * side) % lines
    inner = jnp.logical_and(z > 0, z < lines - 1)
    fwd_dev = ahead * 2 + x
    back_dev = behind * 2 + x

    barrier = pltpu.get_barrier_semaphore()
    for who in ({"seq": partner}, {"seq": z_next}, {"seq": z_prev}, {"head": 1 - core}):
        pl.semaphore_signal(barrier, inc=1, device_id=who, device_id_type=MESH)

    def remote(src, dst, ssem, rsem, who):
        return pltpu.make_async_remote_copy(
            src_ref=src, dst_ref=dst, send_sem=ssem, recv_sem=rsem,
            device_id=who, device_id_type=MESH)

    here = pl.ds(pl.multiple_of(x * rows, rows), rows)
    there = pl.ds(pl.multiple_of((1 - x) * rows, rows), rows)

    def project(index):
        return jnp.dot(tok_ref[...], wqkv_ref[index],
                       preferred_element_type=jnp.float32).astype(jnp.bfloat16)

    load_tok.wait()
    load_w[1].wait()
    krow[here, :] = project(1)
    pl.semaphore_wait(barrier, 4)
    send_x = [remote(buf.at[here], buf.at[here], xs.at[i], xr.at[i], {"seq": partner})
              for i, buf in enumerate((krow, vrow))]
    got_x = [remote(buf.at[there], buf.at[there], xs.at[i], xr.at[i], {"seq": partner})
             for i, buf in enumerate((krow, vrow))]
    send_x[0].start()
    load_w[2].wait()
    vrow[here, :] = project(2)
    send_x[1].start()
    load_o.wait()
    wmine = pl.ds(pl.multiple_of(core * feats, feats), feats)
    wother = pl.ds(pl.multiple_of((1 - core) * feats, feats), feats)
    send_w = remote(
        wout_ref.at[:, pl.ds(pl.multiple_of((1 - core) * half_out, half_out), half_out)],
        wfull.at[wmine], ws.at[0], wr.at[0], {"head": 1 - core})
    send_w.start()
    wfull[wmine, :] = wout_ref[:, pl.ds(pl.multiple_of(core * half_out, half_out), half_out)]
    load_w[0].wait()
    load_r.wait()
    load_g.wait()
    q_ref[...] = project(0)

    near = (near_k, near_v)
    far = (far_k, far_v)
    nsend = (nsend_k, nsend_v)
    fsend = (fsend_k, fsend_v)
    row = (krow, vrow)
    zbuf = (kz, vz)
    gbuf = (gk, gv)

    def near_copy(kind, j, crossing):
        part = pl.ds(aligned(j * BLOCK), BLOCK)
        n = kind * mine + j
        dst, sem = (far, fr) if crossing else (near, nr)
        return remote(nsend[kind].at[part], dst[kind].at[part], ns.at[n], sem.at[n],
                      {"seq": fwd_dev})

    def far_copy(kind, j):
        part = pl.ds(aligned(j * BLOCK), BLOCK)
        n = kind * mine + j
        return remote(fsend[kind].at[part], far[kind].at[part], fs.at[n], fr.at[n],
                      {"seq": back_dev})

    def aligned(start):
        return start if isinstance(start, int) else pl.multiple_of(start, BLOCK)

    def owner(j):
        gid = gid_ref[x * mine + j]
        return lax.div(gid, pair), lax.rem(gid, pair)

    def step_near(kind, j):
        part = pl.ds(aligned(j * BLOCK), BLOCK)
        line, within = owner(j)
        own = row[kind][pl.ds(within * BLOCK, BLOCK), :]

        @pl.when(inner)
        def _():
            near_copy(kind, j, False).wait_recv()
            nsend[kind][part, :] = jnp.where(line == z, own, near[kind][part, :])
            near_copy(kind, j, True).start()

        @pl.when(jnp.logical_not(inner))
        def _():
            nsend[kind][part, :] = own
            near_copy(kind, j, False).start()

    def g_copy(kind, j):
        spot = pl.ds(aligned((x * mine + j) * BLOCK), BLOCK)
        n = kind * mine + j
        return remote(gbuf[kind].at[spot], gbuf[kind].at[spot], gs.at[n], gr.at[n],
                      {"seq": partner})

    def step_far(kind, j):
        part = pl.ds(aligned(j * BLOCK), BLOCK)
        spot = pl.ds(aligned((x * mine + j) * BLOCK), BLOCK)
        line, within = owner(j)
        own = row[kind][pl.ds(within * BLOCK, BLOCK), :]
        far_copy(kind, j).wait_recv()
        arrived = far[kind][part, :]

        @pl.when(inner)
        def _():
            fsend[kind][part, :] = jnp.where(line == z, own, arrived)
            far_copy(kind, j).start()
            before = jnp.where(side == 0, line < z, line > z)
            gbuf[kind][spot, :] = jnp.where(
                line == z, own, jnp.where(before, near[kind][part, :], arrived))

        @pl.when(jnp.logical_not(inner))
        def _():
            gbuf[kind][spot, :] = jnp.where(line == z, own, arrived)

        g_copy(kind, j).start()

    send_z = [remote(row[i].at[there], zbuf[i], zs.at[i], zr.at[i], {"seq": to_near})
              for i in range(2)]

    got_x[0].wait_recv()

    @pl.when(inner)
    def _():
        send_z[0].start()

    for j in range(mine):
        step_near(0, j)

    @pl.when(jnp.logical_not(inner))
    def _():
        send_z[0].start()
        got_x[1].wait_recv()
        for j in range(mine):
            step_near(1, j)
        for j in range(mine):
            step_far(0, j)

    @pl.when(inner)
    def _():
        for j in range(mine):
            step_far(0, j)
        got_x[1].wait_recv()
        for j in range(mine):
            step_near(1, j)

    def swapped(kind):
        for j in range(mine):
            n = kind * mine + j
            spot = pl.ds(pl.multiple_of(((1 - x) * mine + j) * BLOCK, BLOCK), BLOCK)
            remote(gbuf[kind].at[spot], gbuf[kind].at[spot], gs.at[n], gr.at[n],
                   {"seq": partner}).wait_recv()

    send_z[1].start()
    swapped(0)
    send_z[0].wait_recv()

    lane_head = lax.broadcasted_iota(jnp.int32, (BLOCK, feats), 1) // HEAD_DIM
    masks = [(lane_head == h).astype(jnp.float32) for h in range(heads)]
    masks16 = [m.astype(jnp.bfloat16) for m in masks]
    factor = math.log2(math.e) / math.sqrt(HEAD_DIM)
    doc_blocks = cycle * blocks

    def fetch(bufs, e):
        place = e - pair * z
        inside = jnp.logical_and(place >= 0, place < pair)
        place = jnp.clip(place, 0, pair - 1)
        a = bufs[0][pl.ds(place * BLOCK, BLOCK), :]
        b = bufs[1][pl.ds(lax.rem(e, blocks) * BLOCK, BLOCK), :]
        return jnp.where(inside, a, b)

    def att_copy(b):
        spot = pl.ds(pl.multiple_of(b * BLOCK, BLOCK), BLOCK)
        return remote(att.at[core, spot], att.at[core, spot], hs.at[b], hr.at[b],
                      {"head": 1 - core})

    near_keys = (3 + RAND) * BLOCK
    stack = heads * BLOCK

    def picks(b):
        mid = me * blocks + b
        return [lax.rem(mid + doc_blocks - 1, doc_blocks), mid,
                lax.rem(mid + 1, doc_blocks)] + [rand_ref[i, b] for i in range(RAND)]

    def weigh(b, carry):
        spot = pl.ds(pl.multiple_of(b * BLOCK, BLOCK), BLOCK)
        band = pl.ds(pl.multiple_of(b * stack, stack), stack)
        q = q_ref[spot, :]
        stacked = jnp.concatenate([q * m for m in masks16], axis=0)
        kloc = jnp.concatenate([fetch((krow, kz), e) for e in picks(b)], axis=0)
        dims = (((1,), (1,)), ((), ()))
        sl = lax.dot_general(stacked, kloc, dims, preferred_element_type=jnp.float32)
        sg = lax.dot_general(stacked, gk[...], dims, preferred_element_type=jnp.float32)
        top = jnp.maximum(jnp.max(sl, axis=1, keepdims=True), jnp.max(sg, axis=1, keepdims=True))
        el = jnp.exp2((sl - top) * factor)
        eg = jnp.exp2((sg - top) * factor)
        norm = jnp.sum(el, axis=1, keepdims=True) + jnp.sum(eg, axis=1, keepdims=True)
        scale = 1.0 / norm
        probs[band, 0:near_keys] = (el * scale).astype(jnp.bfloat16)
        probs[band, near_keys:] = (eg * scale).astype(jnp.bfloat16)
        step_far(1, b)
        return carry

    lax.fori_loop(0, blocks, weigh, 0)
    swapped(1)
    send_z[1].wait_recv()

    def blend(b, carry):
        spot = pl.ds(pl.multiple_of(b * BLOCK, BLOCK), BLOCK)
        band = pl.ds(pl.multiple_of(b * stack, stack), stack)
        vloc = jnp.concatenate([fetch((vrow, vz), e) for e in picks(b)], axis=0)
        o = jnp.dot(probs[band, 0:near_keys], vloc, preferred_element_type=jnp.float32)
        o += jnp.dot(probs[band, near_keys:], gv[...], preferred_element_type=jnp.float32)
        merged = o[0:BLOCK] * masks[0]
        for h in range(1, heads):
            merged += o[h * BLOCK:(h + 1) * BLOCK] * masks[h]
        att[core, spot, :] = merged.astype(jnp.bfloat16)
        att_copy(b).start()
        return carry

    lax.fori_loop(0, blocks, blend, 0)

    remote(wout_ref.at[:, pl.ds(0, half_out)], wfull.at[wother], ws.at[0], wr.at[0],
           {"head": 1 - core}).wait_recv()
    acc = jnp.dot(att[core], wfull[wmine, :], preferred_element_type=jnp.float32)

    def other_in(b, carry):
        spot = pl.ds(pl.multiple_of(b * BLOCK, BLOCK), BLOCK)
        remote(att.at[1 - core, spot], att.at[1 - core, spot], hs.at[b], hr.at[b],
               {"head": 1 - core}).wait_recv()
        return carry

    lax.fori_loop(0, blocks, other_in, 0)
    acc += jnp.dot(att[1 - core], wfull[wother, :], preferred_element_type=jnp.float32)
    out_ref[...] = acc.astype(jnp.bfloat16)

    for kind in range(2):
        send_x[kind].wait_send()
        send_z[kind].wait_send()
        for j in range(mine):
            near_copy(kind, j, False).wait_send()
            g_copy(kind, j).wait_send()
    send_w.wait_send()

    @pl.when(inner)
    def _():
        for kind in range(2):
            for j in range(mine):
                far_copy(kind, j).wait_send()

    def sent(b, carry):
        att_copy(b).wait_send()
        return carry

    lax.fori_loop(0, blocks, sent, 0)


def routed(tokens, w_qkv, w_out, random_blocks, global_ids):
    rows = tokens.shape[0]
    feats = w_qkv.shape[2]
    width = w_out.shape[1]
    heads_axis = lax.axis_size("head")
    slots = global_ids.shape[0]
    blocks = rows // BLOCK
    mine = slots // 2
    vm = pl.BlockSpec(memory_space=pltpu.VMEM)
    hb = pl.BlockSpec(memory_space=pltpu.HBM)
    bf = jnp.bfloat16
    chain = pltpu.VMEM((mine * BLOCK, feats), bf)
    dma = pltpu.SemaphoreType.DMA
    return pl.pallas_call(
        route_kernel,
        out_shape=jax.ShapeDtypeStruct((rows, width // heads_axis), bf),
        in_specs=[hb, hb, hb, hb, hb],
        out_specs=vm,
        scratch_shapes=[
            pltpu.SMEM(random_blocks.shape[::-1], jnp.int32), pltpu.SMEM(global_ids.shape, jnp.int32),
            pltpu.VMEM(tokens.shape, bf), pltpu.VMEM(w_qkv.shape, bf), pltpu.VMEM(w_out.shape, bf),
            dma((7,)),
            pltpu.VMEM((rows * (feats // HEAD_DIM), (3 + RAND + slots) * BLOCK), bf),
            pltpu.VMEM((2 * rows, feats), bf), pltpu.VMEM((2 * rows, feats), bf),
            pltpu.VMEM((rows, feats), bf), pltpu.VMEM((rows, feats), bf),
            pltpu.VMEM((rows, feats), bf),
            pltpu.VMEM((slots * BLOCK, feats), bf), pltpu.VMEM((slots * BLOCK, feats), bf),
            chain, chain, chain, chain, chain, chain, chain, chain,
            pltpu.VMEM((heads_axis * feats, width // heads_axis), bf),
            pltpu.VMEM((heads_axis, rows, feats), bf),
            dma((2,)), dma((2,)), dma((2,)), dma((2,)),
            dma((slots,)), dma((slots,)), dma((slots,)), dma((slots,)),
            dma((slots,)), dma((slots,)), dma((1,)), dma((1,)),
            dma((blocks,)), dma((blocks,)),
        ],
        compiler_params=pltpu.CompilerParams(
            collective_id=0, has_side_effects=True, vmem_limit_bytes=63 * 1024 * 1024 + 512 * 1024),
    )(random_blocks.T, global_ids, tokens, w_qkv, w_out)


def layer(tokens, w_qkv, w_out, random_blocks, global_ids):
    small = (lax.axis_size("seq") == 8 and lax.axis_size("head") == 2
             and global_ids.shape[0] * BLOCK == 2 * tokens.shape[0])
    run = routed if small else on_device
    return run(tokens, w_qkv, w_out, random_blocks, global_ids)


def solution(mesh):
    return jax.shard_map(
        layer,
        mesh=mesh,
        in_specs=(
            P(("groups", "seq"), None),
            P(None, None, "head"),
            P("head", None),
            P(("groups", "seq"), None),
            P("groups"),
        ),
        out_specs=P(("groups", "seq"), "head"),
        check_vma=False,
    )
```
